256 devices in a mesh: dp: 16 (over z, core), seq: 16 (over x, y).
Axes of the slice: x: 4, y: 4, z: 8, core: 2. Of those that a mesh axis runs over, the one named last changes fastest.
Arguments:
- queries: bfloat16 [16, 2048, 2560], P('dp', 'seq'), may hold values from -24 to 24
- keys: bfloat16 [16, 2048, 2560], P('dp', 'seq'), may hold values from -24 to 24
- values: bfloat16 [16, 2048, 2560], P('dp', 'seq'), may hold values from -6 to 6
- block_masks: int32 [2, 16, 16], replicated, may hold values from 0 to 1, as said below
- head_kind: int32 [20], replicated, may hold values from 0 to 1
- out_weight: bfloat16 [2560, 5120], P(None, 'dp'), may hold values from -0.125 to 0.125
Outputs:
- attended: bfloat16 [16, 2048, 5120], P('dp', 'seq')
The draws below stay inside these ranges and needn't reach their ends.
Inputs may be any that keep to these rules, and one draw needn't show every extreme that they name: block_masks[0, i, j] is 1 wherever blocks i and j lie in the same frame of 4 blocks, block_masks[1, i, j] wherever i - j is a multiple of 4; the other entries are 0 or 1.
All inputs are finite; a program needn't handle non-finite values.
Results may differ from the reference program's by a relative error of at most 0.0057.
Values may be sent and summed in bfloat16 or wider, within the bound.
A program may use at most 128 MiB of HBM per device.

```python
import math
import jax
import jax.numpy as jnp
from jax import lax

D = 5120
HEADS = 20
HEAD_DIM = 128
FRAME_BLOCKS = 4
VIDEOS = 16
SEQ_LEN = 2048
NB = 16


def draw_queries(key, part):
    key = jax.random.fold_in(key, 11)
    own = jnp.clip(jax.random.normal(key, (VIDEOS, SEQ_LEN, HEADS * HEAD_DIM), jnp.float32), -4.0, 4.0)
    return own.astype(jnp.bfloat16)


def draw_keys(key, part):
    key = jax.random.fold_in(key, 23)
    own = jnp.clip(jax.random.normal(key, (VIDEOS, SEQ_LEN, HEADS * HEAD_DIM), jnp.float32), -4.0, 4.0)
    return own.astype(jnp.bfloat16)


def draw_block_masks(key, part):
    key = jax.random.fold_in(key, 5)
    which = lax.broadcasted_iota(jnp.int32, (2, NB, NB), 0)
    row = lax.broadcasted_iota(jnp.int32, (2, NB, NB), 1)
    column = lax.broadcasted_iota(jnp.int32, (2, NB, NB), 2)
    extra = jax.random.randint(key, (2, NB, NB), 0, 8) == 0
    frame = row // FRAME_BLOCKS == column // FRAME_BLOCKS
    stride = (row - column) % FRAME_BLOCKS == 0
    base = jnp.where(which == 0, frame, stride)
    return jnp.where(base | extra, 1, 0).astype(jnp.int32)


def touch_ends(drawn, own_key, least, high):
    index_at = [jax.random.randint(jax.random.fold_in(own_key, axis), (), 0, length) for axis, length in enumerate(drawn.shape)]
    main_axis = drawn.shape.index(max(drawn.shape))
    beside = index_at[:main_axis] + [(index_at[main_axis] + 1) % drawn.shape[main_axis]] + index_at[main_axis + 1:]
    return drawn.at[tuple(index_at)].set(least).at[tuple(beside)].set(high)


def shard_levels(rng, extent, pieces, smallest, top_value):
    def one(dim, parts):
        draws = jax.random.uniform(jax.random.fold_in(jax.random.fold_in(rng, 6), dim), (parts,), jnp.float32, smallest / len(pieces), top_value / len(pieces))
        return jnp.repeat(jnp.exp(draws), extent[dim] // parts).reshape((-1,) + (1,) * (len(extent) - dim - 1))

    gain = one(*pieces[0])
    for cut in pieces[1:]:
        gain = gain * one(*cut)
    return gain


def centred(rng, shape, scale, limit, shards=(), kind=jnp.bfloat16):
    level = shard_levels(rng, shape, shards, -0.22, 0.18) if shards else 1.0
    values = jax.random.normal(rng, shape, jnp.float32) * scale * level
    return jnp.minimum(jnp.maximum(values, -limit), limit).astype(kind)


def setup_inputs(seed: int = 0) -> dict:
    seeds = jax.random.split(jax.random.key(seed), 7)
    return {
        "queries": draw_queries(jax.random.fold_in(seeds[6], 71), 0),
        "keys": draw_keys(jax.random.fold_in(seeds[6], 71), 0),
        "values": centred(seeds[2], (VIDEOS, SEQ_LEN, HEADS * HEAD_DIM), 1.0, 6.0, ((0, 16), (1, 16))),
        "block_masks": draw_block_masks(jax.random.fold_in(seeds[6], 71), 0),
        "head_kind": touch_ends(jax.random.randint(seeds[4], (HEADS,), 0, 2), jax.random.fold_in(seeds[4], 1), 0, 1).astype(jnp.int32),
        "out_weight": centred(seeds[5], (HEADS * HEAD_DIM, D), (HEADS * HEAD_DIM) ** -0.5, 0.125, ((1, 16),)),
    }


def attend(rows_query, row_start, key_rows, value_rows, allowed):
    count, width = rows_query.shape
    length = key_rows.shape[0]
    blocks = allowed.shape[1]
    block = length // blocks
    step = min(512, count)
    scale = 1.0 / math.sqrt(width)

    def one_block(index):
        start = index * step
        query_block = lax.dynamic_slice_in_dim(rows_query, start, step, 0)
        scores = lax.dot_general(query_block, key_rows, (((1,), (1,)), ((), ())), preferred_element_type=jnp.float32) * scale
        window = lax.dynamic_slice_in_dim(allowed, (row_start + start) // block, step // block, 0)
        tiles = scores.reshape(step // block, block, blocks, block)
        tiles = jnp.where(window[:, None, :, None] == 1, tiles, -jnp.inf)
        scores = tiles.reshape(step, length)
        largest = lax.optimization_barrier(jnp.max(scores, axis=1, keepdims=True))
        powers = jnp.exp(scores - largest)
        weights = (powers / lax.optimization_barrier(jnp.sum(powers, axis=1, keepdims=True))).astype(jnp.bfloat16)
        return jnp.dot(weights, value_rows, preferred_element_type=jnp.float32).astype(jnp.bfloat16)
    outputs = lax.map(one_block, jnp.arange(count // step, dtype=jnp.int32))
    return outputs.reshape(count, width)

def reference(queries, keys, values, block_masks, head_kind, out_weight):

    def one_video(items):
        query_rows, key_rows, value_rows = items
        outputs = []
        for head in range(HEADS):
            first = head * HEAD_DIM
            allowed = jnp.where(head_kind[head] == 0, block_masks[0], block_masks[1])
            outputs.append(attend(query_rows[:, first:first + HEAD_DIM], 0, key_rows[:, first:first + HEAD_DIM], value_rows[:, first:first + HEAD_DIM], allowed))
        heads_out = jnp.concatenate(outputs, axis=1)
        return jnp.dot(heads_out, out_weight, preferred_element_type=jnp.float32).astype(jnp.bfloat16)
    return lax.map(one_video, (queries, keys, values))
```

```python
import functools
import math

import jax
import jax.numpy as jnp
from jax import lax
from jax.experimental import pallas as pl
from jax.experimental.pallas import tpu as pltpu
from jax.sharding import PartitionSpec as P

HD = 128
SIDE = 4
PLANE = 16
DEPTH = 8
HEADS = 20
EXTRA = HEADS - PLANE
SEQ = 2048
ROWS = 128
K = 2560
KQ = K // SIDE
NB = 320
RB = 112
RC = NB - 2 * RB
RH = 64
RCH = RC // 2
QB = 256
NC = 256
MESH = pl.DeviceIdType.MESH
SCALE = math.log2(math.e) / math.sqrt(HD)


def rcopy(src, dst, send, recv, device):
    return pltpu.make_async_remote_copy(
        src_ref=src, dst_ref=dst, send_sem=send, recv_sem=recv,
        device_id=device, device_id_type=MESH,
    )


def arrived(ref, sem):
    pltpu.make_async_copy(ref, ref, sem).wait()


def al(value, unit):
    return pl.multiple_of(value, unit)


def kernel(q_in, k_in, v_in, masks, kinds, w_in, out,
           qb, kb, vb, bias, ob, xb, wb, yb, ys,
           zb_sem, zc_sem, x1_sem, x2_sem, a_sem, o_sem, s_sem, y_sem,
           w_send, a_send, o_send, s_send, y_send, l_sem):
    dp = lax.axis_index("dp")
    me = lax.axis_index("seq")
    z, c = dp // 2, dp % 2
    xi, yi = me // SIDE, me % SIDE
    sib = (z * 2 + 1 - c, me)
    up = (((z + 1) % DEPTH) * 2 + c, me)
    down = (((z + DEPTH - 1) % DEPTH) * 2 + c, me)
    near = (
        ((dp, ((xi + 1) % SIDE) * SIDE + yi), (dp, ((xi + 3) % SIDE) * SIDE + yi)),
        ((dp, xi * SIDE + (yi + 1) % SIDE), (dp, xi * SIDE + (yi + 3) % SIDE)),
    )
    coord = (xi, yi)
    extra = me % 5 == 0
    head1 = PLANE + me // 5

    barrier = pltpu.get_barrier_semaphore()

    @pl.loop(1, PLANE)
    def _(d):
        pl.semaphore_signal(barrier, inc=1, device_id=(dp, (me + d) % PLANE), device_id_type=MESH)

    for device in (up, down, sib):
        pl.semaphore_signal(barrier, inc=1, device_id=device, device_id_type=MESH)
    pl.semaphore_wait(barrier, PLANE + 2)

    def piece(block, kind, quarter, first=0, rows=RB):
        start = al(((z + block) % DEPTH) * NB + kind * RB + first, 16)
        return wb.at[pl.ds(start, rows), pl.ds(al(quarter * KQ, HD), KQ)]

    def deep(block, first, rows):
        start = al(((z + block) % DEPTH) * NB + 2 * RB + first, 16)
        return wb.at[pl.ds(start, rows), :]

    own = pltpu.make_async_copy(w_in, wb.at[pl.ds(al(z * NB, 16), NB), :], l_sem)
    own.start()

    for kind in range(2):
        src = w_in.at[kind * RB:(kind + 1) * RB, pl.ds(al(coord[kind] * KQ, HD), KQ)]
        for way, device in enumerate((up, down)):
            rcopy(src, piece(DEPTH, kind, coord[kind]), w_send, zb_sem.at[0, way, kind], device).start()

    sources = (k_in, q_in, v_in)

    def landing(which, slot, block):
        rows = pl.ds(al(block * ROWS, ROWS), ROWS)
        if which == 2:
            return vb.at[slot, rows, 0:HD]
        return (kb, qb)[which].at[slot, rows, :]

    def whole(which, slot):
        if which == 2:
            return vb.at[slot, :, 0:HD]
        return (kb, qb)[which].at[slot]

    def columns(which, head):
        return sources[which].at[:, pl.ds(al(head * HD, HD), HD)]

    @pl.loop(1, PLANE)
    def _(d):
        to = (me + d) % PLANE
        for which in range(3):
            rcopy(columns(which, to), landing(which, 0, me), a_send, a_sem.at[which, 0], (dp, to)).start()

    for which in range(3):
        pltpu.make_async_copy(columns(which, me), landing(which, 0, me), a_sem.at[which, 0]).start()

    @pl.loop(0, EXTRA)
    def _(j):
        for which in range(3):
            @pl.when(me != 5 * j)
            def _():
                rcopy(columns(which, PLANE + j), landing(which, 1, me), a_send,
                      a_sem.at[which, 1], (dp, 5 * j)).start()

            @pl.when(me == 5 * j)
            def _():
                pltpu.make_async_copy(columns(which, PLANE + j), landing(which, 1, me),
                                      a_sem.at[which, 1]).start()

    for slot in range(2):
        kind = kinds[me if slot == 0 else jnp.where(extra, head1, me)]
        allowed = jnp.where(kind == 0, masks[0], masks[1])
        for block in range(SEQ // HD):
            column = jnp.where(allowed[:, block:block + 1] == 1, 0.0, -jnp.inf)
            bias[slot, :, block * HD:(block + 1) * HD] = jnp.broadcast_to(column, (SEQ // HD, HD))
        vb[slot, :, HD:] = jnp.ones((SEQ, HD), jnp.bfloat16)

    def first_hop(block, slot):
        for kind in range(2):
            for way, device in enumerate(near[kind]):
                part = piece(block, kind, coord[kind])
                rcopy(part, part, w_send, x1_sem.at[slot, kind, way], device).start()

    def second_hop(block, slot):
        for kind in range(2):
            back, ahead = (coord[kind] + 3) % SIDE, (coord[kind] + 1) % SIDE
            arrived(piece(block, kind, back), x1_sem.at[slot, kind, 0])
            part = piece(block, kind, back, 0, RH)
            rcopy(part, part, w_send, x2_sem.at[slot, kind, 0], near[kind][0]).start()
            arrived(piece(block, kind, ahead), x1_sem.at[slot, kind, 1])
            part = piece(block, kind, ahead, RH, RB - RH)
            rcopy(part, part, w_send, x2_sem.at[slot, kind, 1], near[kind][1]).start()

    def last_hop(block, slot):
        for kind in range(2):
            far = (coord[kind] + 2) % SIDE
            arrived(piece(block, kind, far, 0, RH), x2_sem.at[slot, kind, 0])
            arrived(piece(block, kind, far, RH, RB - RH), x2_sem.at[slot, kind, 1])

    blocks = (7, 1, 6, 2, 5, 3, 4)

    def along_z(step):
        for way in range(2):
            block = (DEPTH - step, step)[way]
            for kind in range(2):
                arrived(piece(block, kind, coord[kind]), zb_sem.at[step - 1, way, kind])
                if step < 3 or kind == way:
                    part = piece(block, kind, coord[kind])
                    rcopy(part, part, w_send, zb_sem.at[step, way, kind], (up, down)[way]).start()
            first_hop(block, 2 * (step - 1) + way)

    def deep_z(step):
        for way in range(2):
            block = (DEPTH - step, step)[way]
            arrived(deep(block, 0, RC), zc_sem.at[step - 1, way])
            part = deep(block, 0, RC) if step < 3 else deep(block, way * RCH, RCH)
            rcopy(part, part, w_send, zc_sem.at[step, way], (up, down)[way]).start()

    along_z(1)
    along_z(2)
    along_z(3)
    for way, device in enumerate((up, down)):
        rcopy(w_in.at[2 * RB:NB, :], deep(DEPTH, 0, RC), w_send, zc_sem.at[0, way], device).start()
    for kind in range(2):
        arrived(piece(4, kind, coord[kind]), zb_sem.at[3, kind, kind])
    first_hop(4, 6)

    def attention(slot, head, low, high):
        @pl.loop(low, high)
        def _(i):
            turn = (i + me // 2) % (SEQ // QB)
            rows = pl.ds(al(turn * QB, QB), QB)
            scores = lax.dot_general(qb[slot, rows, :], kb[slot], (((1,), (1,)), ((), ())),
                                     preferred_element_type=jnp.float32)
            powers = []
            for half in range(QB // ROWS):
                part = scores[half * ROWS:(half + 1) * ROWS] + bias[slot, pl.ds(turn * 2 + half, 1), :]
                largest = jnp.max(part, axis=1, keepdims=True)
                powers.append(jnp.exp2((part - largest) * SCALE).astype(jnp.bfloat16))
            total = jnp.dot(jnp.concatenate(powers, axis=0), vb[slot], preferred_element_type=jnp.float32)
            ob[slot, rows, :] = (total[:, :HD] / total[:, HD:]).astype(jnp.bfloat16)
            for half in range(QB // ROWS):
                to = turn * 2 + half
                src = ob.at[slot, pl.ds(al(to * ROWS, ROWS), ROWS), :]
                dst = xb.at[0, :, pl.ds(al(head * HD, HD), HD)]

                @pl.when(to != me)
                def _():
                    rcopy(src, dst, o_send, o_sem, (dp, to)).start()

                @pl.when(to == me)
                def _():
                    pltpu.make_async_copy(src, dst, o_sem).start()

    for which in range(3):
        arrived(whole(which, 0), a_sem.at[which, 0])
    attention(0, me, 0, 4)
    second_hop(blocks[0], 0)
    second_hop(blocks[1], 1)
    deep_z(1)
    attention(0, me, 4, 8)
    second_hop(blocks[2], 2)
    second_hop(blocks[3], 3)

    @pl.when(extra)
    def _():
        for which in range(3):
            arrived(whole(which, 1), a_sem.at[which, 1])
        attention(1, head1, 0, 8)

    deep_z(2)
    second_hop(blocks[4], 4)
    second_hop(blocks[5], 5)
    second_hop(blocks[6], 6)

    arrived(xb.at[0], o_sem)
    swap = rcopy(xb.at[0], xb.at[1], s_send, s_sem, sib)
    swap.start()
    deep_z(3)

    @pl.when(extra)
    def _():
        arrived(wb.at[0:54 * 16, 0:8 * HD], a_send)
        arrived(ob.at[:, 0:15 * ROWS, :], o_send)

    @pl.when(jnp.logical_not(extra))
    def _():
        arrived(wb.at[0:57 * 16, 0:8 * HD], a_send)
        arrived(ob.at[0, 0:15 * ROWS, :], o_send)

    own.wait()
    for slot in range(7):
        last_hop(blocks[slot], slot)
    arrived(deep(4, 0, RCH), zc_sem.at[3, 0])
    arrived(deep(4, RCH, RCH), zc_sem.at[3, 1])
    swap.wait()

    rows = xb[...].reshape(2 * ROWS, K)
    sends = []
    for step in range(DEPTH * NB // NC):
        cols = slice(step * NC, (step + 1) * NC)
        part = lax.dot_general(rows, wb[cols, :], (((1,), (1,)), ((), ())),
                               preferred_element_type=jnp.float32).astype(jnp.bfloat16)
        ys[:, cols] = part[ROWS:]
        send = rcopy(ys.at[:, cols], yb.at[c, :, cols], y_send.at[step], y_sem.at[step], sib)
        send.start()
        sends.append(send)
        yb[c, :, cols] = part[:ROWS]
    for send in sends:
        send.wait()
    for pair in range(DEPTH // 2):
        cols = slice(pair * 2 * NB, (pair + 1) * 2 * NB)
        a, b = yb[0, :, cols], yb[1, :, cols]
        out[:, pair * 4 * NB:(pair + 1) * 4 * NB] = jnp.concatenate(
            [a[:, :NB], b[:, :NB], a[:, NB:], b[:, NB:]], axis=1)
    arrived(wb.at[0:14 * RB + 7 * RC, :], w_send)


def per_device(queries, keys, values, block_masks, head_kind, out_weight):
    anywhere = pl.BlockSpec(memory_space=pl.ANY)
    vmem = pl.BlockSpec(memory_space=pltpu.VMEM)
    smem = pl.BlockSpec(memory_space=pltpu.SMEM)
    dma = pltpu.SemaphoreType.DMA
    bf16 = jnp.bfloat16
    attended = pl.pallas_call(
        kernel,
        out_shape=jax.ShapeDtypeStruct((ROWS, 2 * DEPTH * NB), bf16),
        in_specs=[anywhere, anywhere, anywhere, vmem, smem, anywhere],
        out_specs=vmem,
        scratch_shapes=[
            pltpu.VMEM((2, SEQ, HD), bf16),
            pltpu.VMEM((2, SEQ, HD), bf16),
            pltpu.VMEM((2, SEQ, 2 * HD), bf16),
            pltpu.VMEM((2, SEQ // HD, SEQ), jnp.float32),
            pltpu.VMEM((2, SEQ, HD), bf16),
            pltpu.VMEM((2, ROWS, K), bf16),
            pltpu.VMEM((DEPTH * NB, K), bf16),
            pltpu.VMEM((2, ROWS, DEPTH * NB), bf16),
            pltpu.VMEM((ROWS, DEPTH * NB), bf16),
            dma((4, 2, 2)), dma((4, 2)), dma((7, 2, 2)), dma((7, 2, 2)),
            dma((3, 2)), dma, dma, dma((DEPTH * NB // NC,)),
            dma, dma, dma, dma, dma((DEPTH * NB // NC,)), dma,
        ],
        compiler_params=pltpu.CompilerParams(
            collective_id=0, has_side_effects=True, vmem_limit_bytes=60 * 1024 * 1024),
    )(queries[0], keys[0], values[0], block_masks, head_kind, out_weight.T)
    return attended[None]


def solution(mesh):
    placed = (
        P("dp", "seq", None),
        P("dp", "seq", None),
        P("dp", "seq", None),
        P(),
        P(),
        P(None, "dp"),
    )
    return jax.shard_map(
        per_device, mesh=mesh, in_specs=placed, out_specs=P("dp", "seq", None), check_vma=False
    )
```

```python
import functools
import math

import jax
import jax.numpy as jnp
from jax import lax
from jax.experimental import pallas as pl
from jax.experimental.pallas import tpu as pltpu
from jax.sharding import PartitionSpec as P

HD = 128
SIDE = 4
PLANE = 16
DEPTH = 8
HEADS = 20
EXTRA = HEADS - PLANE
SEQ = 2048
ROWS = 128
K = 2560
KQ = K // SIDE
NB = 320
RB = 112
RC = NB - 2 * RB
RH = 64
RCH = RC // 2
QB = 256
MB = SEQ // HD
BIG = -1e30
NC = 256
MESH = pl.DeviceIdType.MESH
ORDER = ((2, 2), (1, 0), (0, 1), (3, 0), (0, 3), (1, 2), (2, 1), (3, 2), (2, 3), (1, 1), (3, 3), (1, 3), (3, 1),
         (2, 0), (0, 2))
SCALE = math.log2(math.e) / math.sqrt(HD)


def rcopy(src, dst, send, recv, device):
    return pltpu.make_async_remote_copy(
        src_ref=src, dst_ref=dst, send_sem=send, recv_sem=recv,
        device_id=device, device_id_type=MESH,
    )


def arrived(ref, sem):
    pltpu.make_async_copy(ref, ref, sem).wait()


def al(value, unit):
    return pl.multiple_of(value, unit)


def kernel(q_in, k_in, v_in, masks, kinds, w_in, out,
           qb, kb, vb, sb, ob, xb, wb, yb, ys,
           zb_sem, zc_sem, x1_sem, x2_sem, a_sem, o_sem, s_sem, y_sem,
           w_send, a_send, o_send, s_send, y_send, l_sem):
    dp = lax.axis_index("dp")
    me = lax.axis_index("seq")
    z, c = dp // 2, dp % 2
    xi, yi = me // SIDE, me % SIDE
    sib = (z * 2 + 1 - c, me)
    up = (((z + 1) % DEPTH) * 2 + c, me)
    down = (((z + DEPTH - 1) % DEPTH) * 2 + c, me)
    near = (
        ((dp, ((xi + 1) % SIDE) * SIDE + yi), (dp, ((xi + 3) % SIDE) * SIDE + yi)),
        ((dp, xi * SIDE + (yi + 1) % SIDE), (dp, xi * SIDE + (yi + 3) % SIDE)),
    )
    coord = (xi, yi)
    extra = yi == (xi + 2 * c) % SIDE
    head1 = PLANE + xi

    barrier = pltpu.get_barrier_semaphore()

    @pl.loop(1, PLANE)
    def _(d):
        pl.semaphore_signal(barrier, inc=1, device_id=(dp, (me + d) % PLANE), device_id_type=MESH)

    for device in (up, down, sib):
        pl.semaphore_signal(barrier, inc=1, device_id=device, device_id_type=MESH)
    own = pltpu.make_async_copy(w_in, wb.at[pl.ds(al(z * NB, 16), NB), :], l_sem)
    own.start()

    block = lax.broadcasted_iota(jnp.int32, (SEQ, HD), 0) // HD
    lane = lax.broadcasted_iota(jnp.int32, (SEQ, HD), 1)
    unit = jnp.where(block == lane, 1.0, 0.0).astype(jnp.bfloat16)
    for slot in range(2):
        kind = kinds[me if slot == 0 else jnp.where(extra, head1, me)]
        allowed = jnp.where(kind == 0, masks[0], masks[1])
        entries = jnp.where(allowed == 1, 0.0, BIG).astype(jnp.bfloat16)
        kb[slot, :, HD:] = unit
        vb[slot, :, HD:] = jnp.ones((SEQ, HD), jnp.bfloat16)
        qb[slot, :, HD:] = jnp.zeros((SEQ, HD), jnp.bfloat16)
        for row in range(MB):
            qb[slot, row * HD:(row + 1) * HD, HD:HD + MB] = jnp.broadcast_to(entries[row:row + 1], (HD, MB))

    pl.semaphore_wait(barrier, PLANE + 2)

    def piece(block, kind, quarter, first=0, rows=RB):
        start = al(((z + block) % DEPTH) * NB + kind * RB + first, 16)
        return wb.at[pl.ds(start, rows), pl.ds(al(quarter * KQ, HD), KQ)]

    def deep(block, first, rows):
        start = al(((z + block) % DEPTH) * NB + 2 * RB + first, 16)
        return wb.at[pl.ds(start, rows), :]

    for kind in range(2):
        src = w_in.at[kind * RB:(kind + 1) * RB, pl.ds(al(coord[kind] * KQ, HD), KQ)]
        for way, device in enumerate((up, down)):
            rcopy(src, piece(DEPTH, kind, coord[kind]), w_send, zb_sem.at[0, way, kind], device).start()

    sources = (k_in, q_in, v_in)

    def landing(which, slot, block):
        rows = pl.ds(al(block * ROWS, ROWS), ROWS)
        return (kb, qb, vb)[which].at[slot, rows, 0:HD]

    def whole(which, slot):
        return (kb, qb, vb)[which].at[slot, :, 0:HD]

    def columns(which, head):
        return sources[which].at[:, pl.ds(al(head * HD, HD), HD)]

    for dx, dy in ORDER:
        to = ((xi + dx) % SIDE) * SIDE + (yi + dy) % SIDE
        for which in range(3):
            rcopy(columns(which, to), landing(which, 0, me), a_send, a_sem.at[which, 0], (dp, to)).start()

    for which in range(3):
        pltpu.make_async_copy(columns(which, me), landing(which, 0, me), a_sem.at[which, 0]).start()

    for j in range(EXTRA):
        to = j * SIDE + (j + 2 * c) % SIDE
        for which in range(3):
            @pl.when(me != to)
            def _():
                rcopy(columns(which, PLANE + j), landing(which, 1, me), a_send,
                      a_sem.at[which, 1], (dp, to)).start()

            @pl.when(me == to)
            def _():
                pltpu.make_async_copy(columns(which, PLANE + j), landing(which, 1, me),
                                      a_sem.at[which, 1]).start()

    def first_hop(block, slot):
        for kind in range(2):
            for way, device in enumerate(near[kind]):
                part = piece(block, kind, coord[kind])
                rcopy(part, part, w_send, x1_sem.at[slot, kind, way], device).start()

    def second_hop(block, slot):
        for kind in range(2):
            back, ahead = (coord[kind] + 3) % SIDE, (coord[kind] + 1) % SIDE
            arrived(piece(block, kind, back), x1_sem.at[slot, kind, 0])
            part = piece(block, kind, back, 0, RH)
            rcopy(part, part, w_send, x2_sem.at[slot, kind, 0], near[kind][0]).start()
            arrived(piece(block, kind, ahead), x1_sem.at[slot, kind, 1])
            part = piece(block, kind, ahead, RH, RB - RH)
            rcopy(part, part, w_send, x2_sem.at[slot, kind, 1], near[kind][1]).start()

    def last_hop(block, slot):
        for kind in range(2):
            far = (coord[kind] + 2) % SIDE
            arrived(piece(block, kind, far, 0, RH), x2_sem.at[slot, kind, 0])
            arrived(piece(block, kind, far, RH, RB - RH), x2_sem.at[slot, kind, 1])

    blocks = (7, 1, 6, 2, 5, 3, 4)

    def along_z(step):
        for way in range(2):
            block = (DEPTH - step, step)[way]
            for kind in range(2):
                arrived(piece(block, kind, coord[kind]), zb_sem.at[step - 1, way, kind])
                if step < 3 or kind == way:
                    part = piece(block, kind, coord[kind])
                    rcopy(part, part, w_send, zb_sem.at[step, way, kind], (up, down)[way]).start()
            first_hop(block, 2 * (step - 1) + way)

    def deep_z(step):
        for way in range(2):
            block = (DEPTH - step, step)[way]
            arrived(deep(block, 0, RC), zc_sem.at[step - 1, way])
            part = deep(block, 0, RC) if step < 3 else deep(block, way * RCH, RCH)
            rcopy(part, part, w_send, zc_sem.at[step, way], (up, down)[way]).start()

    def deep_first():
        for way, device in enumerate((up, down)):
            rcopy(w_in.at[2 * RB:NB, :], deep(DEPTH, 0, RC), w_send, zc_sem.at[0, way], device).start()

    def along_z4():
        for kind in range(2):
            arrived(piece(4, kind, coord[kind]), zb_sem.at[3, kind, kind])
        first_hop(4, 6)

    steps = SEQ // QB

    def rows_of(i):
        turn = (i + me // 2) % steps
        return turn, pl.ds(al(turn * QB, QB), QB)

    def score(slot, i, place):
        _, rows = rows_of(i)
        sb[place] = lax.dot_general(qb[slot, rows, :], kb[slot], (((1,), (1,)), ((), ())),
                                    preferred_element_type=jnp.float32)

    def attend(slot, i, place):
        head = jnp.where(slot == 0, me, head1)
        turn, rows = rows_of(i)
        scores = sb[place]
        powers = jnp.exp2((scores - jnp.max(scores, axis=1, keepdims=True)) * SCALE).astype(jnp.bfloat16)
        total = jnp.dot(powers, vb[slot], preferred_element_type=jnp.float32)
        ob[slot, rows, :] = (total[:, :HD] / total[:, HD:]).astype(jnp.bfloat16)
        for half in range(QB // ROWS):
            to = turn * 2 + half
            src = ob.at[slot, pl.ds(al(to * ROWS, ROWS), ROWS), :]
            dst = xb.at[0, :, pl.ds(al(head * HD, HD), HD)]

            @pl.when(to != me)
            def _():
                rcopy(src, dst, o_send, o_sem, (dp, to)).start()

            @pl.when(to == me)
            def _():
                pltpu.make_async_copy(src, dst, o_sem).start()

    along_z(1)
    along_z(2)
    along_z(3)
    deep_first()
    along_z4()
    for which in range(3):
        arrived(whole(which, 0), a_sem.at[which, 0])
    score(0, 0, 0)

    last = jnp.where(extra, steps, steps // 2) - 1

    @pl.loop(0, last + 1)
    def _(pair):
        slot, i = pair // (steps // 2), 2 * (pair % (steps // 2))
        score(slot, i + 1, 1)
        attend(slot, i, 0)

        @pl.when(jnp.logical_and(extra, pair == steps // 2 - 1))
        def _():
            for which in range(3):
                arrived(whole(which, 1), a_sem.at[which, 1])

        then = jnp.minimum(pair + 1, last)
        score(then // (steps // 2), 2 * (then % (steps // 2)), 0)
        attend(slot, i + 1, 1)

        @pl.when(pair == 1)
        def _():
            deep_z(1)

        @pl.when(pair == 3)
        def _():
            deep_z(2)

    second_hop(blocks[0], 0)
    second_hop(blocks[1], 1)
    second_hop(blocks[2], 2)
    second_hop(blocks[3], 3)
    arrived(xb.at[0], o_sem)
    swap = rcopy(xb.at[0], xb.at[1], s_send, s_sem, sib)
    swap.start()
    second_hop(blocks[4], 4)
    second_hop(blocks[5], 5)
    second_hop(blocks[6], 6)
    deep_z(3)

    @pl.when(extra)
    def _():
        arrived(wb.at[0:54 * 16, 0:8 * HD], a_send)
        arrived(ob.at[:, 0:15 * ROWS, :], o_send)

    @pl.when(jnp.logical_not(extra))
    def _():
        arrived(wb.at[0:57 * 16, 0:8 * HD], a_send)
        arrived(ob.at[0, 0:15 * ROWS, :], o_send)

    own.wait()
    for slot in range(7):
        last_hop(blocks[slot], slot)
    arrived(deep(4, 0, RCH), zc_sem.at[3, 0])
    arrived(deep(4, RCH, RCH), zc_sem.at[3, 1])
    swap.wait()

    rows = xb[...].reshape(2 * ROWS, K)
    sends = []
    for step in range(DEPTH * NB // NC):
        cols = slice(step * NC, (step + 1) * NC)
        part = lax.dot_general(rows, wb[cols, :], (((1,), (1,)), ((), ())),
                               preferred_element_type=jnp.float32).astype(jnp.bfloat16)
        ys[:, cols] = part[ROWS:]
        send = rcopy(ys.at[:, cols], yb.at[c, :, cols], y_send.at[step], y_sem.at[step], sib)
        send.start()
        sends.append(send)
        yb[c, :, cols] = part[:ROWS]
    for send in sends:
        send.wait()
    for pair in range(DEPTH // 2):
        cols = slice(pair * 2 * NB, (pair + 1) * 2 * NB)
        a, b = yb[0, :, cols], yb[1, :, cols]
        out[:, pair * 4 * NB:(pair + 1) * 4 * NB] = jnp.concatenate(
            [a[:, :NB], b[:, :NB], a[:, NB:], b[:, NB:]], axis=1)
    arrived(wb.at[0:14 * RB + 7 * RC, :], w_send)


def per_device(queries, keys, values, block_masks, head_kind, out_weight):
    anywhere = pl.BlockSpec(memory_space=pl.ANY)
    vmem = pl.BlockSpec(memory_space=pltpu.VMEM)
    smem = pl.BlockSpec(memory_space=pltpu.SMEM)
    dma = pltpu.SemaphoreType.DMA
    bf16 = jnp.bfloat16
    attended = pl.pallas_call(
        kernel,
        out_shape=jax.ShapeDtypeStruct((ROWS, 2 * DEPTH * NB), bf16),
        in_specs=[anywhere, anywhere, anywhere, vmem, smem, anywhere],
        out_specs=vmem,
        scratch_shapes=[
            pltpu.VMEM((2, SEQ, 2 * HD), bf16),
            pltpu.VMEM((2, SEQ, 2 * HD), bf16),
            pltpu.VMEM((2, SEQ, 2 * HD), bf16),
            pltpu.VMEM((2, QB, SEQ), jnp.float32),
            pltpu.VMEM((2, SEQ, HD), bf16),
            pltpu.VMEM((2, ROWS, K), bf16),
            pltpu.VMEM((DEPTH * NB, K), bf16),
            pltpu.VMEM((2, ROWS, DEPTH * NB), bf16),
            pltpu.VMEM((ROWS, DEPTH * NB), bf16),
            dma((4, 2, 2)), dma((4, 2)), dma((7, 2, 2)), dma((7, 2, 2)),
            dma((3, 2)), dma, dma, dma((DEPTH * NB // NC,)),
            dma, dma, dma, dma, dma((DEPTH * NB // NC,)), dma,
        ],
        compiler_params=pltpu.CompilerParams(
            collective_id=0, has_side_effects=True, vmem_limit_bytes=60 * 1024 * 1024),
    )(queries[0], keys[0], values[0], block_masks, head_kind, out_weight.T)
    return attended[None]


def solution(mesh):
    placed = (
        P("dp", "seq", None),
        P("dp", "seq", None),
        P("dp", "seq", None),
        P(),
        P(),
        P(None, "dp"),
    )
    return jax.shard_map(
        per_device, mesh=mesh, in_specs=placed, out_specs=P("dp", "seq", None), check_vma=False
    )
```

```python
import functools
import math

import jax
import jax.numpy as jnp
from jax import lax
from jax.experimental import pallas as pl
from jax.experimental.pallas import tpu as pltpu
from jax.sharding import PartitionSpec as P

HD = 128
SIDE = 4
PLANE = 16
DEPTH = 8
HEADS = 20
EXTRA = HEADS - PLANE
SEQ = 2048
ROWS = 128
K = 2560
KQ = K // SIDE
NB = 320
RB = 112
RC = NB - 2 * RB
RH = 64
RCH = RC // 2
QB = 256
MB = SEQ // HD
BIG = -1e30
MESH = pl.DeviceIdType.MESH
ORDER = ((2, 2), (1, 0), (0, 1), (3, 0), (0, 3), (1, 2), (2, 1), (3, 2), (2, 3), (1, 1), (3, 3), (1, 3), (3, 1),
         (2, 0), (0, 2))
SCALE = math.log2(math.e) / math.sqrt(HD)


def rcopy(src, dst, send, recv, device):
    return pltpu.make_async_remote_copy(
        src_ref=src, dst_ref=dst, send_sem=send, recv_sem=recv,
        device_id=device, device_id_type=MESH,
    )


def arrived(ref, sem):
    pltpu.make_async_copy(ref, ref, sem).wait()


def al(value, unit):
    return pl.multiple_of(value, unit)


def kernel(q_in, k_in, v_in, masks, kinds, w_in, out,
           qb, kb, vb, sb, ob, xb, wb, yb, ys,
           zb_sem, zc_sem, x1_sem, x2_sem, a_sem, o_sem, s_sem, y_sem,
           w_send, a_send, o_send, s_send, y_send, l_sem):
    dp = lax.axis_index("dp")
    me = lax.axis_index("seq")
    z, c = dp // 2, dp % 2
    xi, yi = me // SIDE, me % SIDE
    sib = (z * 2 + 1 - c, me)
    up = (((z + 1) % DEPTH) * 2 + c, me)
    down = (((z + DEPTH - 1) % DEPTH) * 2 + c, me)
    near = (
        ((dp, ((xi + 1) % SIDE) * SIDE + yi), (dp, ((xi + 3) % SIDE) * SIDE + yi)),
        ((dp, xi * SIDE + (yi + 1) % SIDE), (dp, xi * SIDE + (yi + 3) % SIDE)),
    )
    coord = (xi, yi)
    extra = yi == (xi + 2 * c) % SIDE
    head1 = PLANE + xi

    barrier = pltpu.get_barrier_semaphore()

    @pl.loop(1, PLANE)
    def _(d):
        pl.semaphore_signal(barrier, inc=1, device_id=(dp, (me + d) % PLANE), device_id_type=MESH)

    for device in (up, down, sib):
        pl.semaphore_signal(barrier, inc=1, device_id=device, device_id_type=MESH)
    own = pltpu.make_async_copy(w_in, wb.at[pl.ds(al(z * NB, 16), NB), :], l_sem)
    own.start()

    block = lax.broadcasted_iota(jnp.int32, (SEQ, HD), 0) // HD
    lane = lax.broadcasted_iota(jnp.int32, (SEQ, HD), 1)
    unit = jnp.where(block == lane, 1.0, 0.0).astype(jnp.bfloat16)
    for slot in range(2):
        kind = kinds[me if slot == 0 else jnp.where(extra, head1, me)]
        allowed = jnp.where(kind == 0, masks[0], masks[1])
        entries = jnp.where(allowed == 1, 0.0, BIG).astype(jnp.bfloat16)
        kb[slot, :, HD:] = unit
        vb[slot, :, HD:] = jnp.ones((SEQ, HD), jnp.bfloat16)
        qb[slot, :, HD:] = jnp.zeros((SEQ, HD), jnp.bfloat16)
        for row in range(MB):
            qb[slot, row * HD:(row + 1) * HD, HD:HD + MB] = jnp.broadcast_to(entries[row:row + 1], (HD, MB))

    pl.semaphore_wait(barrier, PLANE + 2)

    def piece(block, kind, quarter, first=0, rows=RB):
        start = al(((z + block) % DEPTH) * NB + kind * RB + first, 16)
        return wb.at[pl.ds(start, rows), pl.ds(al(quarter * KQ, HD), KQ)]

    def deep(block, first, rows):
        start = al(((z + block) % DEPTH) * NB + 2 * RB + first, 16)
        return wb.at[pl.ds(start, rows), :]

    for kind in range(2):
        src = w_in.at[kind * RB:(kind + 1) * RB, pl.ds(al(coord[kind] * KQ, HD), KQ)]
        for way, device in enumerate((up, down)):
            rcopy(src, piece(DEPTH, kind, coord[kind]), w_send, zb_sem.at[0, way, kind], device).start()

    sources = (k_in, q_in, v_in)

    def landing(which, slot, block):
        rows = pl.ds(al(block * ROWS, ROWS), ROWS)
        return (kb, qb, vb)[which].at[slot, rows, 0:HD]

    def whole(which, slot):
        return (kb, qb, vb)[which].at[slot, :, 0:HD]

    def columns(which, head):
        return sources[which].at[:, pl.ds(al(head * HD, HD), HD)]

    for dx, dy in ORDER:
        to = ((xi + dx) % SIDE) * SIDE + (yi + dy) % SIDE
        for which in range(3):
            rcopy(columns(which, to), landing(which, 0, me), a_send, a_sem.at[which, 0], (dp, to)).start()

    for which in range(3):
        pltpu.make_async_copy(columns(which, me), landing(which, 0, me), a_sem.at[which, 0]).start()

    for j in range(EXTRA):
        to = j * SIDE + (j + 2 * c) % SIDE
        for which in range(3):
            @pl.when(me != to)
            def _():
                rcopy(columns(which, PLANE + j), landing(which, 1, me), a_send,
                      a_sem.at[which, 1], (dp, to)).start()

            @pl.when(me == to)
            def _():
                pltpu.make_async_copy(columns(which, PLANE + j), landing(which, 1, me),
                                      a_sem.at[which, 1]).start()

    def first_hop(block, slot):
        for kind in range(2):
            for way, device in enumerate(near[kind]):
                part = piece(block, kind, coord[kind])
                rcopy(part, part, w_send, x1_sem.at[slot, kind, way], device).start()

    def second_hop(block, slot):
        for kind in range(2):
            back, ahead = (coord[kind] + 3) % SIDE, (coord[kind] + 1) % SIDE
            arrived(piece(block, kind, back), x1_sem.at[slot, kind, 0])
            part = piece(block, kind, back, 0, RH)
            rcopy(part, part, w_send, x2_sem.at[slot, kind, 0], near[kind][0]).start()
            arrived(piece(block, kind, ahead), x1_sem.at[slot, kind, 1])
            part = piece(block, kind, ahead, RH, RB - RH)
            rcopy(part, part, w_send, x2_sem.at[slot, kind, 1], near[kind][1]).start()

    def last_hop(block, slot):
        for kind in range(2):
            far = (coord[kind] + 2) % SIDE
            arrived(piece(block, kind, far, 0, RH), x2_sem.at[slot, kind, 0])
            arrived(piece(block, kind, far, RH, RB - RH), x2_sem.at[slot, kind, 1])

    blocks = (7, 1, 6, 2, 5, 3, 4)

    def along_z(step):
        for way in range(2):
            block = (DEPTH - step, step)[way]
            for kind in range(2):
                arrived(piece(block, kind, coord[kind]), zb_sem.at[step - 1, way, kind])
                if step < 3 or kind == way:
                    part = piece(block, kind, coord[kind])
                    rcopy(part, part, w_send, zb_sem.at[step, way, kind], (up, down)[way]).start()

    def deep_z(step, half):
        for way in range(2):
            part = deep((DEPTH - step, step)[way], half * RCH, RCH)
            arrived(part, zc_sem.at[step - 1, way, half])
            if step < 3 or half == way:
                rcopy(part, part, w_send, zc_sem.at[step, way, half], (up, down)[way]).start()

    def deep_first():
        for half in range(2):
            for way, device in enumerate((up, down)):
                src = w_in.at[2 * RB + half * RCH:2 * RB + (half + 1) * RCH, :]
                rcopy(src, deep(DEPTH, half * RCH, RCH), w_send, zc_sem.at[0, way, half], device).start()

    def along_z4():
        for kind in range(2):
            arrived(piece(4, kind, coord[kind]), zb_sem.at[3, kind, kind])

    steps = SEQ // QB

    def rows_of(i):
        turn = (i + me // 2) % steps
        return turn, pl.ds(al(turn * QB, QB), QB)

    def score(slot, i, place):
        _, rows = rows_of(i)
        sb[place] = lax.dot_general(qb[slot, rows, :], kb[slot], (((1,), (1,)), ((), ())),
                                    preferred_element_type=jnp.float32)

    def attend(slot, i, place):
        head = jnp.where(slot == 0, me, head1)
        turn, rows = rows_of(i)
        scores = sb[place]
        powers = jnp.exp2((scores - jnp.max(scores, axis=1, keepdims=True)) * SCALE).astype(jnp.bfloat16)
        total = jnp.dot(powers, vb[slot], preferred_element_type=jnp.float32)
        ob[slot, rows, :] = (total[:, :HD] / total[:, HD:]).astype(jnp.bfloat16)
        for half in range(QB // ROWS):
            to = turn * 2 + half
            src = ob.at[slot, pl.ds(al(to * ROWS, ROWS), ROWS), :]
            dst = xb.at[0, :, pl.ds(al(head * HD, HD), HD)]

            @pl.when(to != me)
            def _():
                rcopy(src, dst, o_send, o_sem, (dp, to)).start()

            @pl.when(to == me)
            def _():
                pltpu.make_async_copy(src, dst, o_sem).start()

    along_z(1)
    first_hop(blocks[0], 0)
    first_hop(blocks[1], 1)
    along_z(2)
    first_hop(blocks[2], 2)
    first_hop(blocks[3], 3)
    along_z(3)
    first_hop(blocks[4], 4)
    first_hop(blocks[5], 5)
    deep_first()
    along_z4()
    first_hop(blocks[6], 6)
    for which in range(3):
        arrived(whole(which, 0), a_sem.at[which, 0])
    score(0, 0, 0)

    last = jnp.where(extra, steps, steps // 2) - 1

    @pl.loop(0, last + 1)
    def _(pair):
        slot, i = pair // (steps // 2), 2 * (pair % (steps // 2))
        score(slot, i + 1, 1)
        attend(slot, i, 0)

        @pl.when(jnp.logical_and(extra, pair == steps // 2 - 1))
        def _():
            for which in range(3):
                arrived(whole(which, 1), a_sem.at[which, 1])

        then = jnp.minimum(pair + 1, last)
        score(then // (steps // 2), 2 * (then % (steps // 2)), 0)
        attend(slot, i + 1, 1)

        @pl.when(pair == 1)
        def _():
            deep_z(1, 0)

        @pl.when(pair == 2)
        def _():
            deep_z(1, 1)

        @pl.when(pair == 3)
        def _():
            deep_z(2, 0)

    deep_z(2, 1)
    second_hop(blocks[0], 0)
    second_hop(blocks[1], 1)
    second_hop(blocks[2], 2)
    second_hop(blocks[3], 3)
    arrived(xb.at[0], o_sem)
    swap = rcopy(xb.at[0], xb.at[1], s_send, s_sem, sib)
    swap.start()
    deep_z(3, 0)
    second_hop(blocks[4], 4)
    second_hop(blocks[5], 5)
    own.wait()
    swap.wait()

    rows = xb[...].reshape(2 * ROWS, K)

    def project(slot, block):
        where = (z + block) % DEPTH
        part = lax.dot_general(rows, wb[pl.ds(al(where * NB, 64), NB), :], (((1,), (1,)), ((), ())),
                               preferred_element_type=jnp.float32).astype(jnp.bfloat16)
        ys[slot] = part[ROWS:]
        rcopy(ys.at[slot], yb.at[c, slot], y_send.at[slot], y_sem.at[slot], sib).start()
        yb[c, slot] = part[:ROWS]

    def assemble(slot, block):
        where = (z + block) % DEPTH
        arrived(yb.at[1 - c, slot], y_sem.at[slot])
        out[:, pl.ds(al(where * 2 * NB, HD), 2 * NB)] = jnp.concatenate([yb[0, slot], yb[1, slot]], axis=1)

    project(7, 0)
    last_hop(blocks[0], 0)
    project(0, blocks[0])
    assemble(7, 0)
    deep_z(3, 1)
    second_hop(blocks[6], 6)
    last_hop(blocks[1], 1)
    project(1, blocks[1])
    assemble(0, blocks[0])
    last_hop(blocks[2], 2)
    project(2, blocks[2])
    assemble(1, blocks[1])
    last_hop(blocks[3], 3)
    project(3, blocks[3])
    assemble(2, blocks[2])
    last_hop(blocks[4], 4)
    project(4, blocks[4])
    assemble(3, blocks[3])
    last_hop(blocks[5], 5)
    project(5, blocks[5])
    assemble(4, blocks[4])
    last_hop(blocks[6], 6)
    arrived(deep(4, 0, RCH), zc_sem.at[3, 0, 0])
    arrived(deep(4, RCH, RCH), zc_sem.at[3, 1, 1])
    project(6, blocks[6])
    assemble(5, blocks[5])

    @pl.when(extra)
    def _():
        arrived(wb.at[0:54 * 16, 0:8 * HD], a_send)
        arrived(ob.at[:, 0:15 * ROWS, :], o_send)

    @pl.when(jnp.logical_not(extra))
    def _():
        arrived(wb.at[0:57 * 16, 0:8 * HD], a_send)
        arrived(ob.at[0, 0:15 * ROWS, :], o_send)
    arrived(wb.at[0:14 * RB + 7 * RC, :], w_send)
    assemble(6, blocks[6])
    for slot in range(DEPTH):
        arrived(ys.at[slot], y_send.at[slot])


def per_device(queries, keys, values, block_masks, head_kind, out_weight):
    anywhere = pl.BlockSpec(memory_space=pl.ANY)
    vmem = pl.BlockSpec(memory_space=pltpu.VMEM)
    smem = pl.BlockSpec(memory_space=pltpu.SMEM)
    dma = pltpu.SemaphoreType.DMA
    bf16 = jnp.bfloat16
    attended = pl.pallas_call(
        kernel,
        out_shape=jax.ShapeDtypeStruct((ROWS, 2 * DEPTH * NB), bf16),
        in_specs=[anywhere, anywhere, anywhere, vmem, smem, anywhere],
        out_specs=vmem,
        scratch_shapes=[
            pltpu.VMEM((2, SEQ, 2 * HD), bf16),
            pltpu.VMEM((2, SEQ, 2 * HD), bf16),
            pltpu.VMEM((2, SEQ, 2 * HD), bf16),
            pltpu.VMEM((2, QB, SEQ), jnp.float32),
            pltpu.VMEM((2, SEQ, HD), bf16),
            pltpu.VMEM((2, ROWS, K), bf16),
            pltpu.VMEM((DEPTH * NB, K), bf16),
            pltpu.VMEM((2, DEPTH, ROWS, NB), bf16),
            pltpu.VMEM((DEPTH, ROWS, NB), bf16),
            dma((4, 2, 2)), dma((4, 2, 2)), dma((7, 2, 2)), dma((7, 2, 2)),
            dma((3, 2)), dma, dma, dma((DEPTH,)),
            dma, dma, dma, dma, dma((DEPTH,)), dma,
        ],
        compiler_params=pltpu.CompilerParams(
            collective_id=0, has_side_effects=True, vmem_limit_bytes=60 * 1024 * 1024),
    )(queries[0], keys[0], values[0], block_masks, head_kind, out_weight.T)
    return attended[None]


def solution(mesh):
    placed = (
        P("dp", "seq", None),
        P("dp", "seq", None),
        P("dp", "seq", None),
        P(),
        P(),
        P(None, "dp"),
    )
    return jax.shard_map(
        per_device, mesh=mesh, in_specs=placed, out_specs=P("dp", "seq", None), check_vma=False
    )
```

```python
import functools
import math

import jax
import jax.numpy as jnp
from jax import lax
from jax.experimental import pallas as pl
from jax.experimental.pallas import tpu as pltpu
from jax.sharding import PartitionSpec as P

HD = 128
SIDE = 4
PLANE = 16
DEPTH = 8
HEADS = 20
EXTRA = HEADS - PLANE
SEQ = 2048
ROWS = 128
K = 2560
KQ = K // SIDE
NB = 320
RB = 112
RC = NB - 2 * RB
RH = 64
RCH = RC // 2
QB = 256
MB = SEQ // HD
BIG = -1e30
MESH = pl.DeviceIdType.MESH
ORDER = ((2, 2), (1, 0), (0, 1), (3, 0), (0, 3), (1, 2), (2, 1), (3, 2), (2, 3), (1, 1), (3, 3), (1, 3), (3, 1),
         (2, 0), (0, 2))
SCALE = math.log2(math.e) / math.sqrt(HD)


def rcopy(src, dst, send, recv, device):
    return pltpu.make_async_remote_copy(
        src_ref=src, dst_ref=dst, send_sem=send, recv_sem=recv,
        device_id=device, device_id_type=MESH,
    )


def arrived(ref, sem):
    pltpu.make_async_copy(ref, ref, sem).wait()


def al(value, unit):
    return pl.multiple_of(value, unit)


def kernel(q_in, k_in, v_in, masks, kinds, w_in, result,
           out, r_sem, qb, kb, vb, sb, ob, xb, wb, yb, ys,
           zb_sem, zc_sem, x1_sem, x2_sem, a_sem, o_sem, s_sem, y_sem,
           w_send, a_send, o_send, s_send, y_send, l_sem):
    dp = lax.axis_index("dp")
    me = lax.axis_index("seq")
    z, c = dp // 2, dp % 2
    xi, yi = me // SIDE, me % SIDE
    sib = (z * 2 + 1 - c, me)
    up = (((z + 1) % DEPTH) * 2 + c, me)
    down = (((z + DEPTH - 1) % DEPTH) * 2 + c, me)
    near = (
        ((dp, ((xi + 1) % SIDE) * SIDE + yi), (dp, ((xi + 3) % SIDE) * SIDE + yi)),
        ((dp, xi * SIDE + (yi + 1) % SIDE), (dp, xi * SIDE + (yi + 3) % SIDE)),
    )
    coord = (xi, yi)
    extra = yi == (xi + 2 * c) % SIDE
    head1 = PLANE + xi

    barrier = pltpu.get_barrier_semaphore()

    @pl.loop(1, PLANE)
    def _(d):
        pl.semaphore_signal(barrier, inc=1, device_id=(dp, (me + d) % PLANE), device_id_type=MESH)

    for device in (up, down, sib):
        pl.semaphore_signal(barrier, inc=1, device_id=device, device_id_type=MESH)
    own = pltpu.make_async_copy(w_in, wb.at[pl.ds(al(z * NB, 16), NB), :], l_sem)
    own.start()

    block = lax.broadcasted_iota(jnp.int32, (SEQ, HD), 0) // HD
    lane = lax.broadcasted_iota(jnp.int32, (SEQ, HD), 1)
    unit = jnp.where(block == lane, 1.0, 0.0).astype(jnp.bfloat16)
    for slot in range(2):
        kind = kinds[me if slot == 0 else jnp.where(extra, head1, me)]
        allowed = jnp.where(kind == 0, masks[0], masks[1])
        entries = jnp.where(allowed == 1, 0.0, BIG).astype(jnp.bfloat16)
        kb[slot, :, HD:] = unit
        vb[slot, :, HD:] = jnp.ones((SEQ, HD), jnp.bfloat16)
        qb[slot, :, HD:] = jnp.zeros((SEQ, HD), jnp.bfloat16)
        for row in range(MB):
            qb[slot, row * HD:(row + 1) * HD, HD:HD + MB] = jnp.broadcast_to(entries[row:row + 1], (HD, MB))

    pl.semaphore_wait(barrier, PLANE + 2)

    def piece(block, kind, quarter, first=0, rows=RB):
        start = al(((z + block) % DEPTH) * NB + kind * RB + first, 16)
        return wb.at[pl.ds(start, rows), pl.ds(al(quarter * KQ, HD), KQ)]

    def deep(block, first, rows):
        start = al(((z + block) % DEPTH) * NB + 2 * RB + first, 16)
        return wb.at[pl.ds(start, rows), :]

    for kind in range(2):
        src = w_in.at[kind * RB:(kind + 1) * RB, pl.ds(al(coord[kind] * KQ, HD), KQ)]
        for way, device in enumerate((up, down)):
            rcopy(src, piece(DEPTH, kind, coord[kind]), w_send, zb_sem.at[0, way, kind], device).start()

    sources = (k_in, q_in, v_in)

    def landing(which, slot, block):
        rows = pl.ds(al(block * ROWS, ROWS), ROWS)
        return (kb, qb, vb)[which].at[slot, rows, 0:HD]

    def whole(which, slot):
        return (kb, qb, vb)[which].at[slot, :, 0:HD]

    def columns(which, head):
        return sources[which].at[:, pl.ds(al(head * HD, HD), HD)]

    for dx, dy in ORDER:
        to = ((xi + dx) % SIDE) * SIDE + (yi + dy) % SIDE
        for which in range(3):
            rcopy(columns(which, to), landing(which, 0, me), a_send, a_sem.at[which, 0], (dp, to)).start()

    for which in range(3):
        pltpu.make_async_copy(columns(which, me), landing(which, 0, me), a_sem.at[which, 0]).start()

    for j in range(EXTRA):
        to = j * SIDE + (j + 2 * c) % SIDE
        for which in range(3):
            @pl.when(me != to)
            def _():
                rcopy(columns(which, PLANE + j), landing(which, 1, me), a_send,
                      a_sem.at[which, 1], (dp, to)).start()

            @pl.when(me == to)
            def _():
                pltpu.make_async_copy(columns(which, PLANE + j), landing(which, 1, me),
                                      a_sem.at[which, 1]).start()

    def first_hop(block, slot):
        for kind in range(2):
            for way, device in enumerate(near[kind]):
                part = piece(block, kind, coord[kind])
                rcopy(part, part, w_send, x1_sem.at[slot, kind, way], device).start()

    def second_hop(block, slot):
        for kind in range(2):
            back, ahead = (coord[kind] + 3) % SIDE, (coord[kind] + 1) % SIDE
            arrived(piece(block, kind, back), x1_sem.at[slot, kind, 0])
            part = piece(block, kind, back, 0, RH)
            rcopy(part, part, w_send, x2_sem.at[slot, kind, 0], near[kind][0]).start()
            arrived(piece(block, kind, ahead), x1_sem.at[slot, kind, 1])
            part = piece(block, kind, ahead, RH, RB - RH)
            rcopy(part, part, w_send, x2_sem.at[slot, kind, 1], near[kind][1]).start()

    def last_hop(block, slot):
        for kind in range(2):
            far = (coord[kind] + 2) % SIDE
            arrived(piece(block, kind, far, 0, RH), x2_sem.at[slot, kind, 0])
            arrived(piece(block, kind, far, RH, RB - RH), x2_sem.at[slot, kind, 1])

    blocks = (7, 1, 6, 2, 5, 3, 4)

    def along_z(step):
        for way in range(2):
            block = (DEPTH - step, step)[way]
            for kind in range(2):
                arrived(piece(block, kind, coord[kind]), zb_sem.at[step - 1, way, kind])
                if step < 3 or kind == way:
                    part = piece(block, kind, coord[kind])
                    rcopy(part, part, w_send, zb_sem.at[step, way, kind], (up, down)[way]).start()

    def deep_z(step, half):
        for way in range(2):
            part = deep((DEPTH - step, step)[way], half * RCH, RCH)
            arrived(part, zc_sem.at[step - 1, way, half])
            if step < 3 or half == way:
                rcopy(part, part, w_send, zc_sem.at[step, way, half], (up, down)[way]).start()

    def deep_first():
        for half in range(2):
            for way, device in enumerate((up, down)):
                src = w_in.at[2 * RB + half * RCH:2 * RB + (half + 1) * RCH, :]
                rcopy(src, deep(DEPTH, half * RCH, RCH), w_send, zc_sem.at[0, way, half], device).start()

    def along_z4():
        for kind in range(2):
            arrived(piece(4, kind, coord[kind]), zb_sem.at[3, kind, kind])

    steps = SEQ // QB

    def rows_of(i):
        turn = (i + me // 2) % steps
        return turn, pl.ds(al(turn * QB, QB), QB)

    def score(slot, i, place):
        _, rows = rows_of(i)
        sb[place] = lax.dot_general(qb[slot, rows, :], kb[slot], (((1,), (1,)), ((), ())),
                                    preferred_element_type=jnp.float32)

    def attend(slot, i, place):
        head = jnp.where(slot == 0, me, head1)
        turn, rows = rows_of(i)
        scores = sb[place]
        powers = jnp.exp2((scores - jnp.max(scores, axis=1, keepdims=True)) * SCALE).astype(jnp.bfloat16)
        total = jnp.dot(powers, vb[slot], preferred_element_type=jnp.float32)
        ob[slot, rows, :] = (total[:, :HD] / total[:, HD:]).astype(jnp.bfloat16)
        for half in range(QB // ROWS):
            to = turn * 2 + half
            src = ob.at[slot, pl.ds(al(to * ROWS, ROWS), ROWS), :]
            dst = xb.at[0, :, pl.ds(al(head * HD, HD), HD)]

            @pl.when(to != me)
            def _():
                rcopy(src, dst, o_send, o_sem.at[slot], (dp, to)).start()

            @pl.when(to == me)
            def _():
                pltpu.make_async_copy(src, dst, o_sem.at[slot]).start()

    along_z(1)
    first_hop(blocks[0], 0)
    first_hop(blocks[1], 1)
    along_z(2)
    first_hop(blocks[2], 2)
    first_hop(blocks[3], 3)
    along_z(3)
    first_hop(blocks[4], 4)
    first_hop(blocks[5], 5)
    deep_first()
    along_z4()
    first_hop(blocks[6], 6)
    for which in range(3):
        arrived(whole(which, 0), a_sem.at[which, 0])
    score(0, 0, 0)

    last = jnp.where(extra, steps, steps // 2) - 1

    @pl.loop(0, last + 1)
    def _(pair):
        slot, i = pair // (steps // 2), 2 * (pair % (steps // 2))
        score(slot, i + 1, 1)
        attend(slot, i, 0)

        @pl.when(jnp.logical_and(extra, pair == steps // 2 - 1))
        def _():
            for which in range(3):
                arrived(whole(which, 1), a_sem.at[which, 1])

        then = jnp.minimum(pair + 1, last)
        score(then // (steps // 2), 2 * (then % (steps // 2)), 0)
        attend(slot, i + 1, 1)

        @pl.when(pair == 1)
        def _():
            deep_z(1, 0)

        @pl.when(pair == 2)
        def _():
            deep_z(1, 1)

        @pl.when(pair == 3)
        def _():
            deep_z(2, 0)

    deep_z(2, 1)
    second_hop(blocks[0], 0)
    second_hop(blocks[1], 1)
    second_hop(blocks[2], 2)
    second_hop(blocks[3], 3)
    swaps = []
    for slot, cols in enumerate((slice(0, PLANE * HD), slice(PLANE * HD, K))):
        arrived(xb.at[0, :, cols], o_sem.at[slot])
        swap = rcopy(xb.at[0, :, cols], xb.at[1, :, cols], s_send.at[slot], s_sem.at[slot], sib)
        swap.start()
        swaps.append(swap)
    deep_z(3, 0)
    second_hop(blocks[4], 4)
    second_hop(blocks[5], 5)
    own.wait()
    for swap in swaps:
        swap.wait()

    rows = xb[...].reshape(2 * ROWS, K)

    def project(slot, block):
        where = (z + block) % DEPTH
        part = lax.dot_general(rows, wb[pl.ds(al(where * NB, 64), NB), :], (((1,), (1,)), ((), ())),
                               preferred_element_type=jnp.float32).astype(jnp.bfloat16)
        ys[slot] = part[ROWS:]
        rcopy(ys.at[slot], yb.at[c, slot], y_send.at[slot], y_sem.at[slot], sib).start()
        yb[c, slot] = part[:ROWS]

    def assemble(slot, block):
        where = (z + block) % DEPTH
        arrived(yb.at[1 - c, slot], y_sem.at[slot])
        out[slot] = jnp.concatenate([yb[0, slot], yb[1, slot]], axis=1)
        pltpu.make_async_copy(out.at[slot], result.at[:, pl.ds(al(where * 2 * NB, HD), 2 * NB)], r_sem.at[slot]).start()

    project(7, 0)
    last_hop(blocks[0], 0)
    project(0, blocks[0])
    assemble(7, 0)
    deep_z(3, 1)
    second_hop(blocks[6], 6)
    last_hop(blocks[1], 1)
    project(1, blocks[1])
    assemble(0, blocks[0])
    last_hop(blocks[2], 2)
    project(2, blocks[2])
    assemble(1, blocks[1])
    last_hop(blocks[3], 3)
    project(3, blocks[3])
    assemble(2, blocks[2])
    last_hop(blocks[4], 4)
    project(4, blocks[4])
    assemble(3, blocks[3])
    last_hop(blocks[5], 5)
    project(5, blocks[5])
    assemble(4, blocks[4])
    last_hop(blocks[6], 6)
    arrived(deep(4, 0, RCH), zc_sem.at[3, 0, 0])
    arrived(deep(4, RCH, RCH), zc_sem.at[3, 1, 1])
    project(6, blocks[6])
    assemble(5, blocks[5])

    @pl.when(extra)
    def _():
        arrived(wb.at[0:54 * 16, 0:8 * HD], a_send)
        arrived(ob.at[:, 0:15 * ROWS, :], o_send)

    @pl.when(jnp.logical_not(extra))
    def _():
        arrived(wb.at[0:57 * 16, 0:8 * HD], a_send)
        arrived(ob.at[0, 0:15 * ROWS, :], o_send)
    arrived(wb.at[0:14 * RB + 7 * RC, :], w_send)
    assemble(6, blocks[6])
    for slot in range(DEPTH):
        arrived(ys.at[slot], y_send.at[slot])
        arrived(out.at[slot], r_sem.at[slot])


def per_device(queries, keys, values, block_masks, head_kind, out_weight):
    anywhere = pl.BlockSpec(memory_space=pl.ANY)
    vmem = pl.BlockSpec(memory_space=pltpu.VMEM)
    smem = pl.BlockSpec(memory_space=pltpu.SMEM)
    dma = pltpu.SemaphoreType.DMA
    bf16 = jnp.bfloat16
    attended = pl.pallas_call(
        kernel,
        out_shape=jax.ShapeDtypeStruct((ROWS, 2 * DEPTH * NB), bf16),
        in_specs=[anywhere, anywhere, anywhere, vmem, smem, anywhere],
        out_specs=anywhere,
        scratch_shapes=[
            pltpu.VMEM((DEPTH, ROWS, 2 * NB), bf16), dma((DEPTH,)),
            pltpu.VMEM((2, SEQ, 2 * HD), bf16),
            pltpu.VMEM((2, SEQ, 2 * HD), bf16),
            pltpu.VMEM((2, SEQ, 2 * HD), bf16),
            pltpu.VMEM((2, QB, SEQ), jnp.float32),
            pltpu.VMEM((2, SEQ, HD), bf16),
            pltpu.VMEM((2, ROWS, K), bf16),
            pltpu.VMEM((DEPTH * NB, K), bf16),
            pltpu.VMEM((2, DEPTH, ROWS, NB), bf16),
            pltpu.VMEM((DEPTH, ROWS, NB), bf16),
            dma((4, 2, 2)), dma((4, 2, 2)), dma((7, 2, 2)), dma((7, 2, 2)),
            dma((3, 2)), dma((2,)), dma((2,)), dma((DEPTH,)),
            dma, dma, dma, dma((2,)), dma((DEPTH,)), dma,
        ],
        compiler_params=pltpu.CompilerParams(
            collective_id=0, has_side_effects=True, vmem_limit_bytes=60 * 1024 * 1024),
    )(queries[0], keys[0], values[0], block_masks, head_kind, out_weight.T)
    return attended[None]


def solution(mesh):
    placed = (
        P("dp", "seq", None),
        P("dp", "seq", None),
        P("dp", "seq", None),
        P(),
        P(),
        P(None, "dp"),
    )
    return jax.shard_map(
        per_device, mesh=mesh, in_specs=placed, out_specs=P("dp", "seq", None), check_vma=False
    )
```

```python
import functools
import math

import jax
import jax.numpy as jnp
from jax import lax
from jax.experimental import pallas as pl
from jax.experimental.pallas import tpu as pltpu
from jax.sharding import PartitionSpec as P

HD = 128
SIDE = 4
PLANE = 16
DEPTH = 8
HEADS = 20
EXTRA = HEADS - PLANE
SEQ = 2048
ROWS = 128
K = 2560
KQ = K // SIDE
NB = 320
RB = 112
RC = NB - 2 * RB
RH = 64
RCH = RC // 2
QB = 256
MB = SEQ // HD
BIG = -1e30
MESH = pl.DeviceIdType.MESH
ORDER = ((2, 2), (1, 0), (0, 1), (3, 0), (0, 3), (1, 2), (2, 1), (3, 2), (2, 3), (1, 1), (3, 3), (1, 3), (3, 1),
         (2, 0), (0, 2))
SCALE = math.log2(math.e) / math.sqrt(HD)


def rcopy(src, dst, send, recv, device):
    return pltpu.make_async_remote_copy(
        src_ref=src, dst_ref=dst, send_sem=send, recv_sem=recv,
        device_id=device, device_id_type=MESH,
    )


def arrived(ref, sem):
    pltpu.make_async_copy(ref, ref, sem).wait()


def al(value, unit):
    return pl.multiple_of(value, unit)


def kernel(q_in, k_in, v_in, masks, kinds, w_in, result,
           out, r_sem, qb, kb, vb, sb, ob, xb, wb, yb, ys,
           zb_sem, zc_sem, x1_sem, x2_sem, a_sem, o_sem, s_sem, y_sem,
           w_send, a_send, o_send, s_send, y_send, l_sem):
    dp = lax.axis_index("dp")
    me = lax.axis_index("seq")
    z, c = dp // 2, dp % 2
    xi, yi = me // SIDE, me % SIDE
    sib = (z * 2 + 1 - c, me)
    up = (((z + 1) % DEPTH) * 2 + c, me)
    down = (((z + DEPTH - 1) % DEPTH) * 2 + c, me)
    near = (
        ((dp, ((xi + 1) % SIDE) * SIDE + yi), (dp, ((xi + 3) % SIDE) * SIDE + yi)),
        ((dp, xi * SIDE + (yi + 1) % SIDE), (dp, xi * SIDE + (yi + 3) % SIDE)),
    )
    coord = (xi, yi)
    extra = yi == (xi + 2 * c) % SIDE
    head1 = PLANE + xi

    barrier = pltpu.get_barrier_semaphore()

    @pl.loop(1, PLANE)
    def _(d):
        pl.semaphore_signal(barrier, inc=1, device_id=(dp, (me + d) % PLANE), device_id_type=MESH)

    for device in (up, down, sib):
        pl.semaphore_signal(barrier, inc=1, device_id=device, device_id_type=MESH)
    own = pltpu.make_async_copy(w_in, wb.at[pl.ds(al(z * NB, 16), NB), :], l_sem)
    own.start()

    block = lax.broadcasted_iota(jnp.int32, (SEQ, HD), 0) // HD
    lane = lax.broadcasted_iota(jnp.int32, (SEQ, HD), 1)
    unit = jnp.where(block == lane, 1.0, 0.0).astype(jnp.bfloat16)
    for slot in range(2):
        kind = kinds[me if slot == 0 else jnp.where(extra, head1, me)]
        allowed = jnp.where(kind == 0, masks[0], masks[1])
        entries = jnp.where(allowed == 1, 0.0, BIG).astype(jnp.bfloat16)
        kb[slot, :, HD:] = unit
        vb[slot, :, HD:] = jnp.ones((SEQ, HD), jnp.bfloat16)
        qb[slot, :, HD:] = jnp.zeros((SEQ, HD), jnp.bfloat16)
        for row in range(MB):
            qb[slot, row * HD:(row + 1) * HD, HD:HD + MB] = jnp.broadcast_to(entries[row:row + 1], (HD, MB))

    pl.semaphore_wait(barrier, PLANE + 2)

    def piece(block, kind, quarter, first=0, rows=RB):
        start = al(((z + block) % DEPTH) * NB + kind * RB + first, 16)
        return wb.at[pl.ds(start, rows), pl.ds(al(quarter * KQ, HD), KQ)]

    def deep(block, first, rows):
        start = al(((z + block) % DEPTH) * NB + 2 * RB + first, 16)
        return wb.at[pl.ds(start, rows), :]

    for kind in range(2):
        src = w_in.at[kind * RB:(kind + 1) * RB, pl.ds(al(coord[kind] * KQ, HD), KQ)]
        for way, device in enumerate((up, down)):
            rcopy(src, piece(DEPTH, kind, coord[kind]), w_send, zb_sem.at[0, way, kind], device).start()

    sources = (k_in, q_in, v_in)

    def landing(which, slot, block):
        rows = pl.ds(al(block * ROWS, ROWS), ROWS)
        return (kb, qb, vb)[which].at[slot, rows, 0:HD]

    def whole(which, slot):
        return (kb, qb, vb)[which].at[slot, :, 0:HD]

    def columns(which, head):
        return sources[which].at[:, pl.ds(al(head * HD, HD), HD)]

    for dx, dy in ORDER:
        to = ((xi + dx) % SIDE) * SIDE + (yi + dy) % SIDE
        for which in range(3):
            rcopy(columns(which, to), landing(which, 0, me), a_send, a_sem.at[which, 0], (dp, to)).start()

    for which in range(3):
        pltpu.make_async_copy(columns(which, me), landing(which, 0, me), a_sem.at[which, 0]).start()

    for j in range(EXTRA):
        to = j * SIDE + (j + 2 * c) % SIDE
        for which in range(3):
            @pl.when(me != to)
            def _():
                rcopy(columns(which, PLANE + j), landing(which, 1, me), a_send,
                      a_sem.at[which, 1], (dp, to)).start()

            @pl.when(me == to)
            def _():
                pltpu.make_async_copy(columns(which, PLANE + j), landing(which, 1, me),
                                      a_sem.at[which, 1]).start()

    def first_hop(block, slot):
        for kind in range(2):
            for way, device in enumerate(near[kind]):
                part = piece(block, kind, coord[kind])
                rcopy(part, part, w_send, x1_sem.at[slot, kind, way], device).start()

    def second_hop(block, slot):
        for kind in range(2):
            back, ahead = (coord[kind] + 3) % SIDE, (coord[kind] + 1) % SIDE
            arrived(piece(block, kind, back), x1_sem.at[slot, kind, 0])
            part = piece(block, kind, back, 0, RH)
            rcopy(part, part, w_send, x2_sem.at[slot, kind, 0], near[kind][0]).start()
            arrived(piece(block, kind, ahead), x1_sem.at[slot, kind, 1])
            part = piece(block, kind, ahead, RH, RB - RH)
            rcopy(part, part, w_send, x2_sem.at[slot, kind, 1], near[kind][1]).start()

    def last_hop(block, slot):
        for kind in range(2):
            far = (coord[kind] + 2) % SIDE
            arrived(piece(block, kind, far, 0, RH), x2_sem.at[slot, kind, 0])
            arrived(piece(block, kind, far, RH, RB - RH), x2_sem.at[slot, kind, 1])

    blocks = (7, 1, 6, 2, 5, 3, 4)

    def along_z(step):
        for way in range(2):
            block = (DEPTH - step, step)[way]
            for kind in range(2):
                arrived(piece(block, kind, coord[kind]), zb_sem.at[step - 1, way, kind])
                if step < 3 or kind == way:
                    part = piece(block, kind, coord[kind])
                    rcopy(part, part, w_send, zb_sem.at[step, way, kind], (up, down)[way]).start()

    def deep_z(step, half):
        for way in range(2):
            part = deep((DEPTH - step, step)[way], half * RCH, RCH)
            arrived(part, zc_sem.at[step - 1, way, half])
            if step < 3 or half == way:
                rcopy(part, part, w_send, zc_sem.at[step, way, half], (up, down)[way]).start()

    def deep_first():
        for half in range(2):
            for way, device in enumerate((up, down)):
                src = w_in.at[2 * RB + half * RCH:2 * RB + (half + 1) * RCH, :]
                rcopy(src, deep(DEPTH, half * RCH, RCH), w_send, zc_sem.at[0, way, half], device).start()

    def along_z4():
        for kind in range(2):
            arrived(piece(4, kind, coord[kind]), zb_sem.at[3, kind, kind])

    steps = SEQ // QB

    def rows_of(i):
        turn = (i + me // 2) % steps
        return turn, pl.ds(al(turn * QB, QB), QB)

    def score(slot, i, place):
        _, rows = rows_of(i)
        sb[place] = lax.dot_general(qb[slot, rows, :], kb[slot], (((1,), (1,)), ((), ())),
                                    preferred_element_type=jnp.float32)

    def attend(slot, i, place):
        head = jnp.where(slot == 0, me, head1)
        turn, rows = rows_of(i)
        scores = sb[place]
        powers = jnp.exp2((scores - jnp.max(scores, axis=1, keepdims=True)) * SCALE).astype(jnp.bfloat16)
        total = jnp.dot(powers, vb[slot], preferred_element_type=jnp.float32)
        ob[slot, rows, :] = (total[:, :HD] / total[:, HD:]).astype(jnp.bfloat16)
        for half in range(QB // ROWS):
            to = turn * 2 + half
            src = ob.at[slot, pl.ds(al(to * ROWS, ROWS), ROWS), :]
            dst = xb.at[0, :, pl.ds(al(head * HD, HD), HD)]

            @pl.when(to != me)
            def _():
                rcopy(src, dst, o_send, o_sem.at[slot], (dp, to)).start()

            @pl.when(to == me)
            def _():
                pltpu.make_async_copy(src, dst, o_sem.at[slot]).start()

    along_z(1)
    first_hop(blocks[0], 0)
    first_hop(blocks[1], 1)
    along_z(2)
    first_hop(blocks[2], 2)
    first_hop(blocks[3], 3)
    along_z(3)
    first_hop(blocks[4], 4)
    first_hop(blocks[5], 5)
    deep_first()
    along_z4()
    first_hop(blocks[6], 6)
    for which in range(3):
        arrived(whole(which, 0), a_sem.at[which, 0])
    score(0, 0, 0)

    last = jnp.where(extra, steps, steps // 2) - 1

    @pl.loop(0, last + 1)
    def _(pair):
        slot, i = pair // (steps // 2), 2 * (pair % (steps // 2))
        score(slot, i + 1, 1)
        attend(slot, i, 0)

        @pl.when(jnp.logical_and(extra, pair == steps // 2 - 1))
        def _():
            for which in range(3):
                arrived(whole(which, 1), a_sem.at[which, 1])

        then = jnp.minimum(pair + 1, last)
        score(then // (steps // 2), 2 * (then % (steps // 2)), 0)
        attend(slot, i + 1, 1)

        @pl.when(pair == 1)
        def _():
            deep_z(1, 0)

        @pl.when(pair == 2)
        def _():
            deep_z(1, 1)

        @pl.when(pair == 3)
        def _():
            deep_z(2, 0)

    deep_z(2, 1)
    second_hop(blocks[0], 0)
    second_hop(blocks[1], 1)
    second_hop(blocks[2], 2)
    second_hop(blocks[3], 3)
    swaps = []
    for slot, cols in enumerate((slice(0, PLANE * HD), slice(PLANE * HD, K))):
        arrived(xb.at[0, :, cols], o_sem.at[slot])
        swap = rcopy(xb.at[0, :, cols], xb.at[1, :, cols], s_send.at[slot], s_sem.at[slot], sib)
        swap.start()
        swaps.append(swap)
    deep_z(3, 0)
    deep_z(3, 1)
    second_hop(blocks[4], 4)
    second_hop(blocks[5], 5)
    own.wait()
    for swap in swaps:
        swap.wait()

    rows = xb[...].reshape(2 * ROWS, K)

    def project(slot, block):
        where = (z + block) % DEPTH
        part = lax.dot_general(rows, wb[pl.ds(al(where * NB, 64), NB), :], (((1,), (1,)), ((), ())),
                               preferred_element_type=jnp.float32).astype(jnp.bfloat16)
        ys[slot] = part[ROWS:]
        rcopy(ys.at[slot], yb.at[c, slot], y_send.at[slot], y_sem.at[slot], sib).start()
        yb[c, slot] = part[:ROWS]

    def assemble(slot, block):
        where = (z + block) % DEPTH
        arrived(yb.at[1 - c, slot], y_sem.at[slot])
        out[slot] = jnp.concatenate([yb[0, slot], yb[1, slot]], axis=1)
        pltpu.make_async_copy(out.at[slot], result.at[:, pl.ds(al(where * 2 * NB, HD), 2 * NB)], r_sem.at[slot]).start()

    project(7, 0)
    last_hop(blocks[0], 0)
    project(0, blocks[0])
    assemble(7, 0)
    second_hop(blocks[6], 6)
    last_hop(blocks[1], 1)
    project(1, blocks[1])
    assemble(0, blocks[0])
    last_hop(blocks[2], 2)
    project(2, blocks[2])
    assemble(1, blocks[1])
    last_hop(blocks[3], 3)
    project(3, blocks[3])
    assemble(2, blocks[2])
    last_hop(blocks[4], 4)
    project(4, blocks[4])
    assemble(3, blocks[3])
    last_hop(blocks[5], 5)
    project(5, blocks[5])
    assemble(4, blocks[4])
    last_hop(blocks[6], 6)
    arrived(deep(4, 0, RCH), zc_sem.at[3, 0, 0])
    arrived(deep(4, RCH, RCH), zc_sem.at[3, 1, 1])
    project(6, blocks[6])
    assemble(5, blocks[5])

    @pl.when(extra)
    def _():
        arrived(wb.at[0:54 * 16, 0:8 * HD], a_send)
        arrived(ob.at[:, 0:15 * ROWS, :], o_send)

    @pl.when(jnp.logical_not(extra))
    def _():
        arrived(wb.at[0:57 * 16, 0:8 * HD], a_send)
        arrived(ob.at[0, 0:15 * ROWS, :], o_send)
    arrived(wb.at[0:14 * RB + 7 * RC, :], w_send)
    assemble(6, blocks[6])
    for slot in range(DEPTH):
        arrived(ys.at[slot], y_send.at[slot])
        arrived(out.at[slot], r_sem.at[slot])


def per_device(queries, keys, values, block_masks, head_kind, out_weight):
    anywhere = pl.BlockSpec(memory_space=pl.ANY)
    vmem = pl.BlockSpec(memory_space=pltpu.VMEM)
    smem = pl.BlockSpec(memory_space=pltpu.SMEM)
    dma = pltpu.SemaphoreType.DMA
    bf16 = jnp.bfloat16
    attended = pl.pallas_call(
        kernel,
        out_shape=jax.ShapeDtypeStruct((ROWS, 2 * DEPTH * NB), bf16),
        in_specs=[anywhere, anywhere, anywhere, vmem, smem, anywhere],
        out_specs=anywhere,
        scratch_shapes=[
            pltpu.VMEM((DEPTH, ROWS, 2 * NB), bf16), dma((DEPTH,)),
            pltpu.VMEM((2, SEQ, 2 * HD), bf16),
            pltpu.VMEM((2, SEQ, 2 * HD), bf16),
            pltpu.VMEM((2, SEQ, 2 * HD), bf16),
            pltpu.VMEM((2, QB, SEQ), jnp.float32),
            pltpu.VMEM((2, SEQ, HD), bf16),
            pltpu.VMEM((2, ROWS, K), bf16),
            pltpu.VMEM((DEPTH * NB, K), bf16),
            pltpu.VMEM((2, DEPTH, ROWS, NB), bf16),
            pltpu.VMEM((DEPTH, ROWS, NB), bf16),
            dma((4, 2, 2)), dma((4, 2, 2)), dma((7, 2, 2)), dma((7, 2, 2)),
            dma((3, 2)), dma((2,)), dma((2,)), dma((DEPTH,)),
            dma, dma, dma, dma((2,)), dma((DEPTH,)), dma,
        ],
        compiler_params=pltpu.CompilerParams(
            collective_id=0, has_side_effects=True, vmem_limit_bytes=60 * 1024 * 1024),
    )(queries[0], keys[0], values[0], block_masks, head_kind, out_weight.T)
    return attended[None]


def solution(mesh):
    placed = (
        P("dp", "seq", None),
        P("dp", "seq", None),
        P("dp", "seq", None),
        P(),
        P(),
        P(None, "dp"),
    )
    return jax.shard_map(
        per_device, mesh=mesh, in_specs=placed, out_specs=P("dp", "seq", None), check_vma=False
    )
```

```python
import functools
import math

import jax
import jax.numpy as jnp
from jax import lax
from jax.experimental import pallas as pl
from jax.experimental.pallas import tpu as pltpu
from jax.sharding import PartitionSpec as P

HD = 128
SIDE = 4
PLANE = 16
DEPTH = 8
HEADS = 20
EXTRA = HEADS - PLANE
SEQ = 2048
ROWS = 128
K = 2560
KQ = K // SIDE
NB = 320
RB = 112
RC = NB - 2 * RB
RH = 64
RCH = RC // 2
QB = 256
MB = SEQ // HD
BIG = -1e30
MESH = pl.DeviceIdType.MESH
ORDER = ((2, 2), (1, 0), (0, 1), (3, 0), (0, 3), (1, 2), (2, 1), (3, 2), (2, 3), (1, 1), (3, 3), (1, 3), (3, 1),
         (2, 0), (0, 2))
SCALE = math.log2(math.e) / math.sqrt(HD)


def rcopy(src, dst, send, recv, device):
    return pltpu.make_async_remote_copy(
        src_ref=src, dst_ref=dst, send_sem=send, recv_sem=recv,
        device_id=device, device_id_type=MESH,
    )


def arrived(ref, sem):
    pltpu.make_async_copy(ref, ref, sem).wait()


def al(value, unit):
    return pl.multiple_of(value, unit)


def kernel(q_in, k_in, v_in, masks, kinds, w_in, result,
           out, r_sem, qb, kb, vb, sb, ob, xb, wb, yb, ys,
           zb_sem, zc_sem, x1_sem, x2_sem, a_sem, o_sem, s_sem, y_sem,
           w_send, a_send, o_send, s_send, y_send, l_sem):
    dp = lax.axis_index("dp")
    me = lax.axis_index("seq")
    z, c = dp // 2, dp % 2
    xi, yi = me // SIDE, me % SIDE
    sib = (z * 2 + 1 - c, me)
    up = (((z + 1) % DEPTH) * 2 + c, me)
    down = (((z + DEPTH - 1) % DEPTH) * 2 + c, me)
    near = (
        ((dp, ((xi + 1) % SIDE) * SIDE + yi), (dp, ((xi + 3) % SIDE) * SIDE + yi)),
        ((dp, xi * SIDE + (yi + 1) % SIDE), (dp, xi * SIDE + (yi + 3) % SIDE)),
    )
    coord = (xi, yi)
    extra = yi == (xi + 2 * c) % SIDE
    head1 = PLANE + xi

    barrier = pltpu.get_barrier_semaphore()

    @pl.loop(1, PLANE)
    def _(d):
        pl.semaphore_signal(barrier, inc=1, device_id=(dp, (me + d) % PLANE), device_id_type=MESH)

    for device in (up, down, sib):
        pl.semaphore_signal(barrier, inc=1, device_id=device, device_id_type=MESH)
    own = pltpu.make_async_copy(w_in, wb.at[pl.ds(al(z * NB, 16), NB), :], l_sem)
    own.start()

    block = lax.broadcasted_iota(jnp.int32, (SEQ, HD), 0) // HD
    lane = lax.broadcasted_iota(jnp.int32, (SEQ, HD), 1)
    unit = jnp.where(block == lane, 1.0, 0.0).astype(jnp.bfloat16)
    for slot in range(2):
        kind = kinds[me if slot == 0 else jnp.where(extra, head1, me)]
        allowed = jnp.where(kind == 0, masks[0], masks[1])
        entries = jnp.where(allowed == 1, 0.0, BIG).astype(jnp.bfloat16)
        kb[slot, :, HD:] = unit
        vb[slot, :, HD:] = jnp.ones((SEQ, HD), jnp.bfloat16)
        qb[slot, :, HD:] = jnp.zeros((SEQ, HD), jnp.bfloat16)
        for row in range(MB):
            qb[slot, row * HD:(row + 1) * HD, HD:HD + MB] = jnp.broadcast_to(entries[row:row + 1], (HD, MB))

    pl.semaphore_wait(barrier, PLANE + 2)

    def piece(block, kind, quarter, first=0, rows=RB):
        start = al(((z + block) % DEPTH) * NB + kind * RB + first, 16)
        return wb.at[pl.ds(start, rows), pl.ds(al(quarter * KQ, HD), KQ)]

    def deep(block, first, rows):
        start = al(((z + block) % DEPTH) * NB + 2 * RB + first, 16)
        return wb.at[pl.ds(start, rows), :]

    for kind in range(2):
        src = w_in.at[kind * RB:(kind + 1) * RB, pl.ds(al(coord[kind] * KQ, HD), KQ)]
        for way, device in enumerate((up, down)):
            rcopy(src, piece(DEPTH, kind, coord[kind]), w_send, zb_sem.at[0, way, kind], device).start()

    sources = (k_in, q_in, v_in)

    def landing(which, slot, block):
        rows = pl.ds(al(block * ROWS, ROWS), ROWS)
        return (kb, qb, vb)[which].at[slot, rows, 0:HD]

    def whole(which, slot):
        return (kb, qb, vb)[which].at[slot, :, 0:HD]

    def columns(which, head):
        return sources[which].at[:, pl.ds(al(head * HD, HD), HD)]

    for dx, dy in ORDER:
        to = ((xi + dx) % SIDE) * SIDE + (yi + dy) % SIDE
        for which in range(3):
            rcopy(columns(which, to), landing(which, 0, me), a_send, a_sem.at[which, 0], (dp, to)).start()

    for which in range(3):
        pltpu.make_async_copy(columns(which, me), landing(which, 0, me), a_sem.at[which, 0]).start()

    for j in range(EXTRA):
        to = j * SIDE + (j + 2 * c) % SIDE
        for which in range(3):
            @pl.when(me != to)
            def _():
                rcopy(columns(which, PLANE + j), landing(which, 1, me), a_send,
                      a_sem.at[which, 1], (dp, to)).start()

            @pl.when(me == to)
            def _():
                pltpu.make_async_copy(columns(which, PLANE + j), landing(which, 1, me),
                                      a_sem.at[which, 1]).start()

    def first_hop(block, slot):
        for kind in range(2):
            for way, device in enumerate(near[kind]):
                part = piece(block, kind, coord[kind])
                rcopy(part, part, w_send, x1_sem.at[slot, kind, way], device).start()

    def second_hop(block, slot):
        for kind in range(2):
            back, ahead = (coord[kind] + 3) % SIDE, (coord[kind] + 1) % SIDE
            arrived(piece(block, kind, back), x1_sem.at[slot, kind, 0])
            part = piece(block, kind, back, 0, RH)
            rcopy(part, part, w_send, x2_sem.at[slot, kind, 0], near[kind][0]).start()
            arrived(piece(block, kind, ahead), x1_sem.at[slot, kind, 1])
            part = piece(block, kind, ahead, RH, RB - RH)
            rcopy(part, part, w_send, x2_sem.at[slot, kind, 1], near[kind][1]).start()

    def last_hop(block, slot):
        for kind in range(2):
            far = (coord[kind] + 2) % SIDE
            arrived(piece(block, kind, far, 0, RH), x2_sem.at[slot, kind, 0])
            arrived(piece(block, kind, far, RH, RB - RH), x2_sem.at[slot, kind, 1])

    blocks = (7, 1, 6, 2, 5, 3, 4)

    def along_z(step):
        for way in range(2):
            block = (DEPTH - step, step)[way]
            for kind in range(2):
                arrived(piece(block, kind, coord[kind]), zb_sem.at[step - 1, way, kind])
                if step < 3 or kind == way:
                    part = piece(block, kind, coord[kind])
                    rcopy(part, part, w_send, zb_sem.at[step, way, kind], (up, down)[way]).start()

    def deep_z(step, half):
        for way in range(2):
            part = deep((DEPTH - step, step)[way], half * RCH, RCH)
            arrived(part, zc_sem.at[step - 1, way, half])
            if step < 3 or half == way:
                rcopy(part, part, w_send, zc_sem.at[step, way, half], (up, down)[way]).start()

    def deep_first():
        for half in range(2):
            for way, device in enumerate((up, down)):
                src = w_in.at[2 * RB + half * RCH:2 * RB + (half + 1) * RCH, :]
                rcopy(src, deep(DEPTH, half * RCH, RCH), w_send, zc_sem.at[0, way, half], device).start()

    def along_z4():
        for kind in range(2):
            arrived(piece(4, kind, coord[kind]), zb_sem.at[3, kind, kind])

    steps = SEQ // QB

    def rows_of(i):
        turn = (i + me // 2) % steps
        return turn, pl.ds(al(turn * QB, QB), QB)

    def score(slot, i, place):
        _, rows = rows_of(i)
        sb[place] = lax.dot_general(qb[slot, rows, :], kb[slot], (((1,), (1,)), ((), ())),
                                    preferred_element_type=jnp.float32)

    def attend(slot, i, place):
        head = jnp.where(slot == 0, me, head1)
        turn, rows = rows_of(i)
        scores = sb[place]
        powers = jnp.exp2((scores - jnp.max(scores, axis=1, keepdims=True)) * SCALE).astype(jnp.bfloat16)
        total = jnp.dot(powers, vb[slot], preferred_element_type=jnp.float32)
        ob[slot, rows, :] = (total[:, :HD] / total[:, HD:]).astype(jnp.bfloat16)
        for half in range(QB // ROWS):
            to = turn * 2 + half
            src = ob.at[slot, pl.ds(al(to * ROWS, ROWS), ROWS), :]
            dst = xb.at[0, :, pl.ds(al(head * HD, HD), HD)]

            @pl.when(to != me)
            def _():
                rcopy(src, dst, o_send, o_sem.at[slot], (dp, to)).start()

            @pl.when(to == me)
            def _():
                pltpu.make_async_copy(src, dst, o_sem.at[slot]).start()

    along_z(1)
    first_hop(blocks[0], 0)
    first_hop(blocks[1], 1)
    along_z(2)
    first_hop(blocks[2], 2)
    first_hop(blocks[3], 3)
    along_z(3)
    first_hop(blocks[4], 4)
    first_hop(blocks[5], 5)
    deep_first()
    along_z4()
    first_hop(blocks[6], 6)
    for which in range(3):
        arrived(whole(which, 0), a_sem.at[which, 0])
    score(0, 0, 0)

    last = jnp.where(extra, steps, steps // 2) - 1

    @pl.loop(0, last + 1)
    def _(pair):
        slot, i = pair // (steps // 2), 2 * (pair % (steps // 2))
        score(slot, i + 1, 1)
        attend(slot, i, 0)

        @pl.when(jnp.logical_and(extra, pair == steps // 2 - 1))
        def _():
            for which in range(3):
                arrived(whole(which, 1), a_sem.at[which, 1])

        then = jnp.minimum(pair + 1, last)
        score(then // (steps // 2), 2 * (then % (steps // 2)), 0)
        attend(slot, i + 1, 1)

        @pl.when(pair == 1)
        def _():
            deep_z(1, 0)

        @pl.when(pair == 2)
        def _():
            deep_z(1, 1)

        @pl.when(pair == 3)
        def _():
            deep_z(2, 0)

    deep_z(2, 1)
    second_hop(blocks[0], 0)
    second_hop(blocks[1], 1)
    second_hop(blocks[2], 2)
    second_hop(blocks[3], 3)
    swaps = []
    for slot, cols in enumerate((slice(0, PLANE * HD), slice(PLANE * HD, K))):
        arrived(xb.at[0, :, cols], o_sem.at[slot])
        swap = rcopy(xb.at[0, :, cols], xb.at[1, :, cols], s_send.at[slot], s_sem.at[slot], sib)
        swap.start()
        swaps.append(swap)
    deep_z(3, 0)
    deep_z(3, 1)
    second_hop(blocks[4], 4)
    second_hop(blocks[5], 5)
    own.wait()
    for swap in swaps:
        swap.wait()

    rows = xb[...].reshape(2 * ROWS, K)

    def project(slot, block):
        where = (z + block) % DEPTH
        part = lax.dot_general(rows, wb[pl.ds(al(where * NB, 64), NB), :], (((1,), (1,)), ((), ())),
                               preferred_element_type=jnp.float32).astype(jnp.bfloat16)
        ys[slot] = part[ROWS:]
        rcopy(ys.at[slot], yb.at[c, slot], y_send.at[slot], y_sem.at[slot], sib).start()
        yb[c, slot] = part[:ROWS]

    def assemble(slot, block):
        where = (z + block) % DEPTH
        arrived(yb.at[1 - c, slot], y_sem.at[slot])
        out[slot] = jnp.concatenate([yb[0, slot], yb[1, slot]], axis=1)
        pltpu.make_async_copy(out.at[slot], result.at[:, pl.ds(al(where * 2 * NB, HD), 2 * NB)], r_sem.at[slot]).start()

    second_hop(blocks[6], 6)
    project(7, 0)
    last_hop(blocks[0], 0)
    project(0, blocks[0])
    assemble(7, 0)
    last_hop(blocks[1], 1)
    project(1, blocks[1])
    assemble(0, blocks[0])
    last_hop(blocks[2], 2)
    project(2, blocks[2])
    assemble(1, blocks[1])
    last_hop(blocks[3], 3)
    project(3, blocks[3])
    assemble(2, blocks[2])
    last_hop(blocks[4], 4)
    project(4, blocks[4])
    assemble(3, blocks[3])
    last_hop(blocks[5], 5)
    project(5, blocks[5])
    assemble(4, blocks[4])
    last_hop(blocks[6], 6)
    arrived(deep(4, 0, RCH), zc_sem.at[3, 0, 0])
    arrived(deep(4, RCH, RCH), zc_sem.at[3, 1, 1])
    project(6, blocks[6])
    assemble(5, blocks[5])

    @pl.when(extra)
    def _():
        arrived(wb.at[0:54 * 16, 0:8 * HD], a_send)
        arrived(ob.at[:, 0:15 * ROWS, :], o_send)

    @pl.when(jnp.logical_not(extra))
    def _():
        arrived(wb.at[0:57 * 16, 0:8 * HD], a_send)
        arrived(ob.at[0, 0:15 * ROWS, :], o_send)
    arrived(wb.at[0:14 * RB + 7 * RC, :], w_send)
    assemble(6, blocks[6])
    for slot in range(DEPTH):
        arrived(ys.at[slot], y_send.at[slot])
        arrived(out.at[slot], r_sem.at[slot])


def per_device(queries, keys, values, block_masks, head_kind, out_weight):
    anywhere = pl.BlockSpec(memory_space=pl.ANY)
    vmem = pl.BlockSpec(memory_space=pltpu.VMEM)
    smem = pl.BlockSpec(memory_space=pltpu.SMEM)
    dma = pltpu.SemaphoreType.DMA
    bf16 = jnp.bfloat16
    attended = pl.pallas_call(
        kernel,
        out_shape=jax.ShapeDtypeStruct((ROWS, 2 * DEPTH * NB), bf16),
        in_specs=[anywhere, anywhere, anywhere, vmem, smem, anywhere],
        out_specs=anywhere,
        scratch_shapes=[
            pltpu.VMEM((DEPTH, ROWS, 2 * NB), bf16), dma((DEPTH,)),
            pltpu.VMEM((2, SEQ, 2 * HD), bf16),
            pltpu.VMEM((2, SEQ, 2 * HD), bf16),
            pltpu.VMEM((2, SEQ, 2 * HD), bf16),
            pltpu.VMEM((2, QB, SEQ), jnp.float32),
            pltpu.VMEM((2, SEQ, HD), bf16),
            pltpu.VMEM((2, ROWS, K), bf16),
            pltpu.VMEM((DEPTH * NB, K), bf16),
            pltpu.VMEM((2, DEPTH, ROWS, NB), bf16),
            pltpu.VMEM((DEPTH, ROWS, NB), bf16),
            dma((4, 2, 2)), dma((4, 2, 2)), dma((7, 2, 2)), dma((7, 2, 2)),
            dma((3, 2)), dma((2,)), dma((2,)), dma((DEPTH,)),
            dma, dma, dma, dma((2,)), dma((DEPTH,)), dma,
        ],
        compiler_params=pltpu.CompilerParams(
            collective_id=0, has_side_effects=True, vmem_limit_bytes=60 * 1024 * 1024),
    )(queries[0], keys[0], values[0], block_masks, head_kind, out_weight.T)
    return attended[None]


def solution(mesh):
    placed = (
        P("dp", "seq", None),
        P("dp", "seq", None),
        P("dp", "seq", None),
        P(),
        P(),
        P(None, "dp"),
    )
    return jax.shard_map(
        per_device, mesh=mesh, in_specs=placed, out_specs=P("dp", "seq", None), check_vma=False
    )
```
